32 devices in a mesh: gx: 4 (over x, core), gy: 4 (over z), gz: 2 (over y).
Axes of the slice: x: 2, y: 2, z: 4, core: 2. Of those that a mesh axis runs over, the one named last changes fastest.
Arguments:
- unary: bfloat16 [16, 32, 128, 128], P('gx', 'gy', 'gz'), may hold values from -3 to 3
- compat: float32 [6, 128, 128], replicated, may hold values from -2.5 to 2.5
- saved_first: bfloat16 [6, 16, 32, 128, 128], P(None, 'gx', 'gy', 'gz'), may hold values from 0.25 to 4
- saved_second: bfloat16 [6, 16, 32, 128, 128], P(None, 'gx', 'gy', 'gz'), may hold values from 0.25 to 4
- cotangent: float32 [16, 32, 128, 128], P('gx', 'gy', 'gz'), may hold values from -6 to 6
Outputs:
- grad_unary: float32 [16, 32, 128, 128], P('gx', 'gy', 'gz')
- grad_compat: float32 [6, 128, 128], replicated
The draws below stay inside these ranges and needn't reach their ends.
All inputs are finite; a program needn't handle non-finite values.
Results may differ from the reference program's by a relative error of at most 0.0084.
Values may be sent and summed in bfloat16 or wider, within the bound.
A program may use at most 128 MiB of HBM per device.

```python
import math
import jax
import jax.numpy as jnp
from jax import lax

L = 128
NX = 16
NY = 32
NZ = 128


def level_of(key, shape, cuts, low, top_value):
    loudness, own = 1.0, jax.random.fold_in(key, 6)
    for dim, parts in cuts:
        heights = jnp.exp(jax.random.uniform(jax.random.fold_in(own, dim), (parts,), jnp.float32, low / len(cuts), top_value / len(cuts)))
        loudness = loudness * jnp.repeat(heights, shape[dim] // parts).reshape([-1 if axis == dim else 1 for axis in range(len(shape))])
    return loudness


def scatter_about(stream_key, dims, width, reach, split=(), held_as=jnp.bfloat16):
    array = width * jax.random.normal(stream_key, dims, jnp.float32)
    if split:
        array = array * level_of(stream_key, dims, split, -0.22, 0.18)
    return jnp.clip(array, -reach, reach).astype(held_as)


def setup_inputs(seed: int = 0) -> dict:
    splits = jax.random.split(jax.random.key(seed), 6)
    unary = scatter_about(splits[0], (NX, NY, NZ, L), 1.0, 3.0, ((0, 4), (1, 4), (2, 2)))
    compat = scatter_about(splits[1], (6, L, L), 0.5, 2.5, (), jnp.float32)
    saved_first = jnp.clip(jnp.exp(math.log(4.0) - 2.7725887 * jax.random.uniform(splits[2], (6, NX, NY, NZ, L), jnp.float32) ** level_of(splits[2], (6, NX, NY, NZ, L), ((1, 4), (2, 4), (3, 2)), -0.2, 0.2)), 0.25, 4.0).astype(jnp.bfloat16)
    saved_second = jnp.clip(jnp.exp(math.log(4.0) - 2.7725887 * jax.random.uniform(splits[3], (6, NX, NY, NZ, L), jnp.float32) ** level_of(splits[3], (6, NX, NY, NZ, L), ((1, 4), (2, 4), (3, 2)), -0.2, 0.2)), 0.25, 4.0).astype(jnp.bfloat16)
    cotangent = scatter_about(splits[4], (NX, NY, NZ, L), 1.0, 6.0, ((0, 4), (1, 4), (2, 2)), jnp.float32)
    return dict(unary=unary, compat=compat, saved_first=saved_first, saved_second=saved_second, cotangent=cotangent)


OPPOSE = (1, 0, 3, 2, 5, 4)


def product_except(fields, skipped):
    result = None
    for index in range(6):
        if index in skipped:
            continue
        result = fields[index] if result is None else result * fields[index]
    return result


def send_terms(potential, messages, weights_b):
    labels = potential.shape[-1]
    hidden_b, normal, totals = [], [], []
    for direction in range(6):
        packed = (potential * product_except(messages, (OPPOSE[direction],))).astype(jnp.bfloat16)
        outgoing = jnp.dot(packed.reshape(-1, labels), weights_b[direction], preferred_element_type=jnp.float32).reshape(potential.shape)
        summed = jnp.sum(outgoing, axis=-1, keepdims=True)
        hidden_b.append(packed)
        normal.append(labels * outgoing / summed)
        totals.append(summed)
    return hidden_b, normal, totals


def forward_shift(normal_b):
    result = []
    for axis_dim in range(3):
        plus = normal_b[2 * axis_dim]
        minus = normal_b[2 * axis_dim + 1]
        length = plus.shape[axis_dim]
        ones = jnp.ones_like(lax.slice_in_dim(plus, 0, 1, axis=axis_dim))
        result.append(jnp.concatenate([ones, lax.slice_in_dim(plus, 0, length - 1, axis=axis_dim)], axis=axis_dim))
        result.append(jnp.concatenate([lax.slice_in_dim(minus, 1, length, axis=axis_dim), ones], axis=axis_dim))
    return result


def adjoint_shift(grad_b):
    result = []
    for axis_dim in range(3):
        plus = grad_b[2 * axis_dim]
        minus = grad_b[2 * axis_dim + 1]
        length = plus.shape[axis_dim]
        zeros = jnp.zeros_like(lax.slice_in_dim(plus, 0, 1, axis=axis_dim))
        result.append(jnp.concatenate([lax.slice_in_dim(plus, 1, length, axis=axis_dim), zeros], axis=axis_dim))
        result.append(jnp.concatenate([zeros, lax.slice_in_dim(minus, 0, length - 1, axis=axis_dim)], axis=axis_dim))
    return result


def belief_adjoint(potential, arriving, cotangent):
    labels = potential.shape[-1]
    whole = product_except(arriving, ())
    joint = potential * whole
    summed = jnp.sum(joint, axis=-1, keepdims=True)
    belief = joint / summed
    grad_joint = labels * (cotangent - jnp.sum(cotangent * belief, axis=-1, keepdims=True)) / summed
    grad_potential = grad_joint * whole
    grad_arriving = [(grad_joint * potential * product_except(arriving, (edge,))).astype(jnp.bfloat16) for edge in range(6)]
    return grad_arriving, grad_potential


def normal_adjoint(grad_normal, normal, totals):
    labels = normal.shape[-1]
    inner = jnp.sum(grad_normal * normal, axis=-1, keepdims=True)
    return ((labels / totals) * (grad_normal - inner / labels)).astype(jnp.bfloat16)


def local_adjoint(grad_normal, normal, totals, hidden_b, weights_b):
    labels = normal[0].shape[-1]
    grad_weights, grad_hidden = [], []
    for direction in range(6):
        grad_out = normal_adjoint(grad_normal[direction], normal[direction], totals[direction]).reshape(-1, labels)
        grad_weights.append(jnp.dot(hidden_b[direction].reshape(-1, labels).T, grad_out, preferred_element_type=jnp.float32))
        grad_hidden.append(jnp.dot(grad_out, weights_b[direction].T, preferred_element_type=jnp.float32).reshape(normal[0].shape))
    return jnp.stack(grad_weights), grad_hidden


def potential_terms(grad_hidden, messages):
    total = None
    for direction in range(6):
        term = grad_hidden[direction] * product_except(messages, (OPPOSE[direction],))
        total = term if total is None else total + term
    return total


def message_terms(grad_hidden, potential, messages):
    result = []
    for edge in range(6):
        total = None
        for direction in range(6):
            if direction == OPPOSE[edge]:
                continue
            term = grad_hidden[direction] * product_except(messages, (OPPOSE[direction], edge))
            total = term if total is None else total + term
        result.append((potential * total).astype(jnp.bfloat16))
    return result


def reference(unary, compat, saved_first, saved_second, cotangent):
    potential = jnp.exp(unary.astype(jnp.float32))
    weights = jnp.exp(compat)
    weights_b = weights.astype(jnp.bfloat16)
    first = [saved_first[index].astype(jnp.float32) for index in range(6)]
    second = [saved_second[index].astype(jnp.float32) for index in range(6)]
    hidden_two, normal_two, totals_two = send_terms(potential, second, weights_b)
    arriving = forward_shift([value.astype(jnp.bfloat16) for value in normal_two])
    arriving = [value.astype(jnp.float32) for value in arriving]
    grad_arriving, grad_potential = belief_adjoint(potential, arriving, cotangent)
    grad_normal_two = [value.astype(jnp.float32) for value in adjoint_shift(grad_arriving)]
    weights_two, grad_hidden_two = local_adjoint(grad_normal_two, normal_two, totals_two, hidden_two, weights_b)
    grad_potential = grad_potential + potential_terms(grad_hidden_two, second)
    grad_second = message_terms(grad_hidden_two, potential, second)
    hidden_one, normal_one, totals_one = send_terms(potential, first, weights_b)
    grad_normal_one = [value.astype(jnp.float32) for value in adjoint_shift(grad_second)]
    weights_one, grad_hidden_one = local_adjoint(grad_normal_one, normal_one, totals_one, hidden_one, weights_b)
    grad_potential = grad_potential + potential_terms(grad_hidden_one, first)
    grad_unary = potential * grad_potential
    grad_compat = weights * (weights_two + weights_one)
    return grad_unary, grad_compat
```

```python
import functools

import jax
import jax.numpy as jnp
from jax import lax
from jax.experimental import pallas as pl
from jax.experimental.pallas import tpu as pltpu
from jax.sharding import PartitionSpec as P

OPPOSE = (1, 0, 3, 2, 5, 4)
AXES = ("gx", "gy", "gz")
MESH = pl.DeviceIdType.MESH
F32 = jnp.float32
BF16 = jnp.bfloat16
CHUNK = 16


def recip(value):
    guess = pl.reciprocal(value, approx=True)
    return guess * (2.0 - value * guess)


def leave_one_out(start, fields):
    before = [start]
    for index in range(5):
        before.append(before[-1] * fields[index])
    after = fields[5]
    result = [None] * 6
    result[5] = before[5]
    for index in range(4, -1, -1):
        result[index] = before[index] * after
        if index:
            after = after * fields[index]
    return result


class Halo:
    def __init__(self, x_ref, y_ref, z_ref, zhalo_ref, zsend_ref, forward, shape):
        self.x, self.y, self.z, self.zhalo, self.zsend = x_ref, y_ref, z_ref, zhalo_ref, zsend_ref
        self.shape = shape
        self.step = [(-1 if d % 2 == 0 else 1) * (1 if forward else -1) for d in range(6)]

    def own(self, d):
        return 1 if self.step[d] < 0 else 0

    def read(self, d):
        return 0 if self.step[d] < 0 else 1

    def at_own(self, d, x, y):
        if d < 2:
            return self.x.at[d, x + self.own(d), y]
        if d < 4:
            return self.y.at[d - 2, x, y + self.own(d)]
        return self.z.at[d - 4, x, y]

    def at_shifted(self, d, x, y):
        if d < 2:
            return self.x.at[d, x + self.read(d), y]
        return self.y.at[d - 2, x, y + self.read(d)]

    def halo(self, d):
        X, Y, Z, L = self.shape
        if d < 2:
            return self.x.at[d, 0 if self.step[d] < 0 else X]
        if d < 4:
            return self.y.at[d - 2, :, 0 if self.step[d] < 0 else Y]
        return self.zhalo.at[d - 4]

    def face(self, d):
        X, Y, Z, L = self.shape
        if d < 2:
            return self.x.at[d, X if self.step[d] < 0 else 0]
        if d < 4:
            return self.y.at[d - 2, :, Y if self.step[d] < 0 else 0]
        return self.zsend.at[d - 4]


def kernel(
    sizes, scatter, other,
    unary_h, compat, first_h, second_h, cot_h,
    out_h, grad_compat,
    unary, first, second, cot, phi, out, hb, inv, hidden_grad, acc, psib, wide,
    nx, ny, nz, nzs, nzh, nzo, ax, ay, az, azh, azo, bx, by, bz, bzh, bzo,
    rs_src, rs_recv, os_buf, ag_buf,
    in_sem, send_sem, recv_sem, rs_send, rs_recv_sem, os_send, os_recv_sem, ag_send, ag_recv_sem,
):
    X, Y, Z, L = shape = phi.shape
    me = {axis: lax.axis_index(axis) for axis in AXES}

    def target(**changed):
        return tuple(changed.get(axis, me[axis]) for axis in AXES)

    inner_count = sizes[scatter[1]]
    group = sizes[scatter[0]] * inner_count
    mine = me[scatter[0]] * inner_count + me[scatter[1]]
    others = sizes[other]
    rows = 6 * L // group

    def member(index):
        return target(**{scatter[0]: index // inner_count, scatter[1]: index % inner_count})

    loads = [
        pltpu.make_async_copy(src, dst, in_sem.at[i])
        for i, (src, dst) in enumerate(
            ((unary_h, unary), (second_h, second), (cot_h, cot), (first_h, first))
        )
    ]
    for load in loads:
        load.start()

    barrier = pltpu.get_barrier_semaphore()
    for k in range(1, group):
        pl.semaphore_signal(barrier, inc=1, device_id=member((mine + k) % group), device_id_type=MESH)
    for k in range(1, others):
        pl.semaphore_signal(
            barrier, inc=1, device_id=target(**{other: (me[other] + k) % others}), device_id_type=MESH
        )

    for d in range(6):
        rounded = jnp.exp(compat[d]).astype(BF16)
        psib[d] = rounded
        wide[d, :, :L] = rounded
        sums = jnp.sum(rounded.astype(F32), axis=1, keepdims=True)
        wide[d, :, L:] = jnp.broadcast_to(sums, (L, L)).astype(BF16)

    N = Halo(nx, ny, nz, nzh, nzo, True, shape)
    A = Halo(ax, ay, az, azh, azo, False, shape)
    B = Halo(bx, by, bz, bzh, bzo, False, shape)

    def exchange(field, number):
        plan = []
        for d in range(6):
            axis = AXES[d // 2]
            count = sizes[axis]
            place = me[axis]
            up = field.step[d] < 0
            goal = place + 1 if up else place - 1
            sends = place < count - 1 if up else place > 0
            gets = place > 0 if up else place < count - 1
            copy = pltpu.make_async_remote_copy(
                src_ref=field.face(d),
                dst_ref=field.halo(d),
                send_sem=send_sem.at[number, d],
                recv_sem=recv_sem.at[number, d],
                device_id=target(**{axis: goal}),
                device_id_type=MESH,
            )
            plan.append((sends, gets, copy))
        return plan

    def start(plan, field, value):
        for d, (sends, gets, copy) in enumerate(plan):
            @pl.when(sends)
            def _():
                copy.start()

            @pl.when(jnp.logical_not(gets))
            def _():
                spot = field.halo(d)
                spot[...] = jnp.full(spot.shape, value, spot.dtype)

    def wait_recv(plan):
        for sends, gets, copy in plan:
            @pl.when(gets)
            def _():
                copy.wait_recv()

    def wait_send(plan):
        for sends, gets, copy in plan:
            @pl.when(sends)
            def _():
                copy.wait_send()

    def columns(lo, hi, step):
        def one(i, carry):
            step(i // Y, i % Y)
            return carry

        lax.fori_loop(lo * Y, hi * Y, one, 0)

    def planes(lo, hi, step):
        def one(x, carry):
            step(x)
            return carry

        lax.fori_loop(lo, hi, one, 0)

    cuts = [pl.ds(c * CHUNK, CHUNK) for c in range(Z // CHUNK)]
    last = len(cuts) - 1

    def send_terms(messages, shifted):
        def hidden(x, y):
            for cut in cuts:
                if shifted:
                    potential = jnp.exp(unary[x, y, cut].astype(F32))
                    phi[x, y, cut] = potential
                else:
                    potential = phi[x, y, cut]
                fields = [messages[e, x, y, cut].astype(F32) for e in range(6)]
                products = leave_one_out(potential, fields)
                for e in range(6):
                    hb[OPPOSE[e], x, y, cut] = products[e].astype(BF16)

        columns(0, X, hidden)

        def outgoing(x):
            for d in range(6):
                both = jnp.dot(
                    hb[d, x].reshape(Y * Z, L), wide[d], preferred_element_type=F32
                )
                scale = L * recip(both[:, L:])
                inv[d, x] = scale.reshape(Y, Z, L)
                normal = (both[:, :L] * scale).reshape(Y, Z, L)
                if d < 2:
                    nx[d, x + N.own(d)] = normal.astype(BF16)
                elif d < 4:
                    ny[d - 2, x, pl.ds(N.own(d), Y)] = normal.astype(BF16)
                else:
                    nz[d - 4, x] = normal.astype(BF16)
                    if shifted:
                        for y in range(Y):
                            edge = Z - 1 if d == 4 else 0
                            nzo[d - 4, pl.ds(x * Y + y, 1)] = normal[y, edge:edge + 1]
                            nzs[d - 4, x, y] = pltpu.roll(
                                normal[y], 1 if d == 4 else Z - 1, 0
                            ).astype(BF16)

        planes(0, X, outgoing)

    def belief(x, y):
        spot = pl.ds(x * Y + y, 1)
        for c, cut in enumerate(cuts):
            fields = [N.at_shifted(d, x, y)[cut].astype(F32) for d in range(4)]
            row = lax.broadcasted_iota(jnp.int32, (CHUNK, L), 0)
            low = nzs[0, x, y, cut].astype(F32)
            if c == 0:
                low = jnp.where(row == 0, nzh[0, spot].astype(BF16).astype(F32), low)
            high = nzs[1, x, y, cut].astype(F32)
            if c == last:
                high = jnp.where(row == CHUNK - 1, nzh[1, spot].astype(BF16).astype(F32), high)
            fields += [low, high]
            before = [phi[x, y, cut]]
            for e in range(6):
                before.append(before[-1] * fields[e])
            joint = before[6]
            target_grad = cot[x, y, cut]
            scale = recip(jnp.sum(joint, axis=-1, keepdims=True))
            mean = jnp.sum(target_grad * joint, axis=-1, keepdims=True) * scale
            grad = (target_grad - mean) * (L * scale)
            out[x, y, cut] = grad * joint
            after = grad
            for e in range(5, -1, -1):
                value = before[e] * after
                A.at_own(e, x, y)[cut] = value.astype(BF16)
                if e == 4 and c == 0:
                    azo[0, spot] = value[0:1]
                if e == 5 and c == last:
                    azo[1, spot] = value[CHUNK - 1:CHUNK]
                after = after * fields[e]

    def grad_out(field):
        def one(x, y):
            row = lax.broadcasted_iota(jnp.int32, (Z, L), 0)
            spot = pl.ds(x * Y + y, 1)
            for d in range(6):
                if d < 4:
                    grad = field.at_shifted(d, x, y)[...].astype(F32)
                else:
                    value = field.z[d - 4, x, y].astype(F32)
                    halo = field.zhalo[d - 4, spot]
                    if d == 4:
                        grad = jnp.where(row == Z - 1, halo, pltpu.roll(value, Z - 1, 0))
                    else:
                        grad = jnp.where(row == 0, halo, pltpu.roll(value, 1, 0))
                place = N.at_own(d, x, y)
                inner = jnp.sum(grad * place[...].astype(F32), axis=-1, keepdims=True) * (1.0 / L)
                place[...] = (inv[d, x, y] * (grad - inner)).astype(BF16)

        return one

    def go_plane(d, x):
        if d < 2:
            value = nx[d, x + N.own(d)]
        elif d < 4:
            value = ny[d - 2, x, pl.ds(N.own(d), Y)]
        else:
            value = nz[d - 4, x]
        return value.reshape(Y * Z, L)

    def weight_terms(x):
        for d in range(6):
            acc[d] += lax.dot_general(
                hb[d, x].reshape(Y * Z, L), go_plane(d, x), (((0,), (0,)), ((), ())),
                preferred_element_type=F32,
            )

    def hidden_terms(x):
        for d in range(6):
            hidden_grad[d] = lax.dot_general(
                go_plane(d, x), psib[d], (((1,), (1,)), ((), ())), preferred_element_type=F32
            ).reshape(Y, Z, L)

    def adjoint(messages, field):
        def one(x, y):
            spot = pl.ds(x * Y + y, 1)
            for c, cut in enumerate(cuts):
                fields = [messages[e, x, y, cut].astype(F32) for e in range(6)]
                grads = [hidden_grad[OPPOSE[e], y, cut] for e in range(6)]
                before = [phi[x, y, cut]]
                slope = [None]
                for e in range(6):
                    part = before[e] * grads[e]
                    slope.append(part if e == 0 else slope[e] * fields[e] + part)
                    before.append(before[e] * fields[e] if e < 5 else None)
                out[x, y, cut] += slope[6]
                if field is None:
                    continue
                after, fall = None, None
                for e in range(5, -1, -1):
                    if e == 5:
                        value = slope[5]
                        after, fall = fields[5], grads[5]
                    else:
                        value = before[e] * fall
                        if e:
                            value = value + slope[e] * after
                            fall = fall * fields[e] + after * grads[e]
                            after = after * fields[e]
                    field.at_own(e, x, y)[cut] = value.astype(BF16)
                    if e == 4 and c == 0:
                        field.zsend[0, spot] = value[0:1]
                    if e == 5 and c == last:
                        field.zsend[1, spot] = value[CHUNK - 1:CHUNK]

        return one

    loads[0].wait()
    loads[1].wait()
    send_terms(second, True)
    pl.semaphore_wait(barrier, group + others - 2)
    one = exchange(N, 0)
    start(one, N, 1.0)
    acc[...] = jnp.zeros_like(acc)
    loads[2].wait()
    wait_recv(one)
    columns(0, X, belief)
    two = exchange(A, 1)
    start(two, A, 0.0)
    wait_send(one)
    wait_recv(two)

    def second_back(x):
        each = grad_out(A)
        lax.fori_loop(0, Y, lambda y, carry: (each(x, y), carry)[1], 0)
        weight_terms(x)
        hidden_terms(x)
        combine = adjoint(second, B)
        lax.fori_loop(0, Y, lambda y, carry: (combine(x, y), carry)[1], 0)

    planes(0, X, second_back)
    three = exchange(B, 2)
    start(three, B, 0.0)
    wait_send(two)

    loads[3].wait()
    send_terms(first, False)
    wait_recv(three)
    columns(0, X, grad_out(B))
    planes(0, X, weight_terms)
    wait_send(three)

    def first_back(x):
        hidden_terms(x)
        combine = adjoint(first, None)
        lax.fori_loop(0, Y, lambda y, carry: (combine(x, y), carry)[1], 0)

    rs_src[...] = acc[...].reshape(group, rows, L).astype(BF16)
    scatters = []
    for k in range(1, group):
        goal = (mine + k) % group
        scatters.append(
            pltpu.make_async_remote_copy(
                src_ref=rs_src.at[goal], dst_ref=rs_recv.at[k - 1],
                send_sem=rs_send.at[k - 1], recv_sem=rs_recv_sem.at[k - 1],
                device_id=member(goal), device_id_type=MESH,
            )
        )
    for copy in scatters:
        copy.start()
    planes(0, X // 2, first_back)
    total = rs_src[mine].astype(F32)
    for k, copy in enumerate(scatters):
        copy.wait_recv()
        total = total + rs_recv[k].astype(F32)
    os_buf[me[other]] = total.astype(BF16)
    trades = []
    for k in range(1, others):
        goal = (me[other] + k) % others
        source = (me[other] + others - k) % others
        here = pltpu.make_async_remote_copy(
            src_ref=os_buf.at[me[other]], dst_ref=os_buf.at[me[other]],
            send_sem=os_send.at[k - 1], recv_sem=os_recv_sem.at[k - 1],
            device_id=target(**{other: goal}), device_id_type=MESH,
        )
        trades.append(here)
    for copy in trades:
        copy.start()
    planes(X // 2, X // 2 + X // 4, first_back)
    for copy in trades:
        copy.wait_recv()
    total = os_buf[0].astype(F32)
    for k in range(1, others):
        total = total + os_buf[k].astype(F32)
    ag_buf[mine] = total.astype(BF16)
    gathers = []
    for k in range(1, group):
        gathers.append(
            pltpu.make_async_remote_copy(
                src_ref=ag_buf.at[mine], dst_ref=ag_buf.at[mine],
                send_sem=ag_send.at[k - 1], recv_sem=ag_recv_sem.at[k - 1],
                device_id=member((mine + k) % group), device_id_type=MESH,
            )
        )
    for copy in gathers:
        copy.start()
    planes(X // 2 + X // 4, X, first_back)
    store = pltpu.make_async_copy(out, out_h, in_sem.at[4])
    store.start()
    for copy in gathers:
        copy.wait_recv()
    grad_compat[...] = jnp.exp(compat[...]) * ag_buf[...].astype(F32).reshape(6, L, L)
    for copy in scatters + trades + gathers:
        copy.wait_send()
    store.wait()


def body(sizes, unary, compat, saved_first, saved_second, cotangent):
    X, Y, Z, L = unary.shape
    scatter, other = ("gx", "gz"), "gy"
    if (6 * L) % (16 * sizes["gx"] * sizes["gz"]):
        scatter, other = ("gy", "gz"), "gx"
    group = sizes[scatter[0]] * sizes[scatter[1]]
    others = sizes[other]
    rows = 6 * L // group
    field = (X, Y, Z, L)

    def halo_set(extra):
        return [
            pltpu.VMEM((2, X + 1, Y, Z, L), BF16),
            pltpu.VMEM((2, X, Y + 1, Z, L), BF16),
            pltpu.VMEM((2, X, Y, Z, L), BF16),
        ] + extra + [pltpu.VMEM((2, X * Y, L), F32), pltpu.VMEM((2, X * Y, L), F32)]

    dma = pltpu.SemaphoreType.DMA
    return pl.pallas_call(
        functools.partial(kernel, sizes, scatter, other),
        out_shape=(
            jax.ShapeDtypeStruct(field, F32),
            jax.ShapeDtypeStruct((6, L, L), F32),
        ),
        in_specs=[
            pl.BlockSpec(memory_space=pl.ANY),
            pl.BlockSpec(memory_space=pltpu.VMEM),
            pl.BlockSpec(memory_space=pl.ANY),
            pl.BlockSpec(memory_space=pl.ANY),
            pl.BlockSpec(memory_space=pl.ANY),
        ],
        out_specs=(pl.BlockSpec(memory_space=pl.ANY), pl.BlockSpec(memory_space=pltpu.VMEM)),
        scratch_shapes=[
            pltpu.VMEM(field, BF16),
            pltpu.VMEM((6,) + field, BF16),
            pltpu.VMEM((6,) + field, BF16),
            pltpu.VMEM(field, F32),
            pltpu.VMEM(field, F32),
            pltpu.VMEM(field, F32),
            pltpu.VMEM((6,) + field, BF16),
            pltpu.VMEM((6,) + field, F32),
            pltpu.VMEM((6, Y, Z, L), F32),
            pltpu.VMEM((6, L, L), F32),
            pltpu.VMEM((6, L, L), BF16),
            pltpu.VMEM((6, L, 2 * L), BF16),
        ]
        + halo_set([pltpu.VMEM((2, X, Y, Z, L), BF16)])
        + halo_set([])
        + halo_set([])
        + [
            pltpu.VMEM((group, rows, L), BF16),
            pltpu.VMEM((group - 1, rows, L), BF16),
            pltpu.VMEM((others, rows, L), BF16),
            pltpu.VMEM((group, rows, L), BF16),
            dma((5,)),
            dma((3, 6)),
            dma((3, 6)),
            dma((group - 1,)),
            dma((group - 1,)),
            dma((others - 1,)),
            dma((others - 1,)),
            dma((group - 1,)),
            dma((group - 1,)),
        ],
        compiler_params=pltpu.CompilerParams(
            collective_id=0, has_side_effects=True, vmem_limit_bytes=64 * 1024 * 1024 - 65536
        ),
    )(unary, compat, saved_first, saved_second, cotangent)


def solution(mesh):
    sizes = dict(mesh.shape)
    placed = (
        P("gx", "gy", "gz", None),
        P(),
        P(None, "gx", "gy", "gz", None),
        P(None, "gx", "gy", "gz", None),
        P("gx", "gy", "gz", None),
    )
    return jax.shard_map(
        functools.partial(body, sizes),
        mesh=mesh,
        in_specs=placed,
        out_specs=(P("gx", "gy", "gz", None), P()),
        check_vma=False,
    )
```

```python
import functools

import jax
import jax.numpy as jnp
from jax import lax
from jax.experimental import pallas as pl
from jax.experimental.pallas import tpu as pltpu
from jax.sharding import PartitionSpec as P

OPPOSE = (1, 0, 3, 2, 5, 4)
AXES = ("gx", "gy", "gz")
MESH = pl.DeviceIdType.MESH
F32 = jnp.float32
BF16 = jnp.bfloat16
CHUNK = 16


def recip(value):
    guess = pl.reciprocal(value, approx=True)
    return guess * (2.0 - value * guess)


def leave_one_out(start, fields):
    before = [start]
    for index in range(5):
        before.append(before[-1] * fields[index])
    after = fields[5]
    result = [None] * 6
    result[5] = before[5]
    for index in range(4, -1, -1):
        result[index] = before[index] * after
        if index:
            after = after * fields[index]
    return result


class Halo:
    def __init__(self, x_ref, y_ref, z_ref, zhalo_ref, zsend_ref, forward, shape):
        self.x, self.y, self.z, self.zhalo, self.zsend = x_ref, y_ref, z_ref, zhalo_ref, zsend_ref
        self.shape = shape
        self.step = [(-1 if d % 2 == 0 else 1) * (1 if forward else -1) for d in range(6)]

    def own(self, d):
        return 1 if self.step[d] < 0 else 0

    def read(self, d):
        return 0 if self.step[d] < 0 else 1

    def at_own(self, d, x, y):
        if d < 2:
            return self.x.at[d, x + self.own(d), y]
        if d < 4:
            return self.y.at[d - 2, x, y + self.own(d)]
        return self.z.at[d - 4, x, y]

    def at_shifted(self, d, x, y):
        if d < 2:
            return self.x.at[d, x + self.read(d), y]
        return self.y.at[d - 2, x, y + self.read(d)]

    def plane(self, d, x):
        X, Y, Z, L = self.shape
        if d < 2:
            return self.x.at[d, x + self.own(d)]
        if d < 4:
            return self.y.at[d - 2, x, pl.ds(self.own(d), Y)]
        return self.z.at[d - 4, x]

    def halo(self, d):
        X, Y, Z, L = self.shape
        if d < 2:
            return self.x.at[d, 0 if self.step[d] < 0 else X]
        if d < 4:
            return self.y.at[d - 2, :, 0 if self.step[d] < 0 else Y]
        return self.zhalo.at[d - 4]

    def face(self, d):
        X, Y, Z, L = self.shape
        if d < 2:
            return self.x.at[d, X if self.step[d] < 0 else 0]
        if d < 4:
            return self.y.at[d - 2, :, Y if self.step[d] < 0 else 0]
        return self.zsend.at[d - 4]


class Flat:
    def __init__(self, ref):
        self.ref = ref

    def at_own(self, d, x, y):
        return self.ref.at[d, x, y]

    def plane(self, d, x):
        return self.ref.at[d, x]


def kernel(
    early, sizes, scatter, other,
    unary_h, compat, first_h, second_h, cot_h,
    out_h, grad_compat,
    unary, first, second, cot, phi, out, hb, inv, hidden_grad, acc, psib, wide,
    nx, ny, nz, nzs, nzh, nzo, ax, ay, az, azh, azo, bx, by, bz, bzh, bzo,
    rs_src, rs_recv, os_buf, ag_buf, mean,
    in_sem, send_sem, recv_sem, rs_send, rs_recv_sem, os_send, os_recv_sem, ag_send, ag_recv_sem,
    *more,
):
    X, Y, Z, L = shape = phi.shape
    me = {axis: lax.axis_index(axis) for axis in AXES}

    def target(**changed):
        return tuple(changed.get(axis, me[axis]) for axis in AXES)

    inner_count = sizes[scatter[1]]
    group = sizes[scatter[0]] * inner_count
    mine = me[scatter[0]] * inner_count + me[scatter[1]]
    others = sizes[other]
    rows = 6 * L // group

    def member(index):
        return target(**{scatter[0]: index // inner_count, scatter[1]: index % inner_count})

    loads = [
        pltpu.make_async_copy(src, dst, in_sem.at[i])
        for i, (src, dst) in enumerate(
            ((unary_h, unary), (second_h, second), (cot_h, cot), (first_h, first))
        )
    ]
    for load in loads:
        load.start()

    barrier = pltpu.get_barrier_semaphore()
    for k in range(1, group):
        pl.semaphore_signal(barrier, inc=1, device_id=member((mine + k) % group), device_id_type=MESH)
    for k in range(1, others):
        pl.semaphore_signal(
            barrier, inc=1, device_id=target(**{other: (me[other] + k) % others}), device_id_type=MESH
        )

    for d in range(6):
        rounded = jnp.exp(compat[d]).astype(BF16)
        psib[d] = rounded
        wide[d, :, :L] = rounded
        sums = jnp.sum(rounded.astype(F32), axis=1, keepdims=True)
        wide[d, :, L:] = jnp.broadcast_to(sums, (L, L)).astype(BF16)

    mean[...] = jnp.full((L, L), 1.0 / L, BF16)

    N = Halo(nx, ny, nz, nzh, nzo, True, shape)
    A = Halo(ax, ay, az, azh, azo, False, shape)
    B = Halo(bx, by, bz, bzh, bzo, False, shape)

    def exchange(field, number):
        plan = []
        for d in range(6):
            axis = AXES[d // 2]
            count = sizes[axis]
            place = me[axis]
            up = field.step[d] < 0
            goal = place + 1 if up else place - 1
            sends = place < count - 1 if up else place > 0
            gets = place > 0 if up else place < count - 1
            copy = pltpu.make_async_remote_copy(
                src_ref=field.face(d),
                dst_ref=field.halo(d),
                send_sem=send_sem.at[number, d],
                recv_sem=recv_sem.at[number, d],
                device_id=target(**{axis: goal}),
                device_id_type=MESH,
            )
            plan.append((sends, gets, copy))
        return plan

    def start(plan, field, value, which):
        for d in which:
            sends, gets, copy = plan[d]

            @pl.when(sends)
            def _():
                copy.start()

            @pl.when(jnp.logical_not(gets))
            def _():
                spot = field.halo(d)
                spot[...] = jnp.full(spot.shape, value, spot.dtype)

    def wait_recv(plan):
        for sends, gets, copy in plan:
            @pl.when(gets)
            def _():
                copy.wait_recv()

    def wait_send(plan):
        for sends, gets, copy in plan:
            @pl.when(sends)
            def _():
                copy.wait_send()

    def planes(lo, hi, step, stride=1):
        def one(x, carry):
            step(x * stride)
            return carry

        lax.fori_loop(lo, hi, one, 0)

    def columns(lo, hi, step, stride=1, width=1):
        pieces = Y // width

        def one(i, carry):
            for j in range(width):
                step((i // pieces) * stride, (i % pieces) * width + j)
            return carry

        lax.fori_loop(lo * pieces, hi * pieces, one, 0)

    inside, rims = (1, X - 1), (0, 2)

    cuts = [pl.ds(c * CHUNK, CHUNK) for c in range(Z // CHUNK)]
    last = len(cuts) - 1

    def hidden(messages, store, fresh):
        def one(x, y):
            for cut in cuts:
                if fresh:
                    potential = jnp.exp(unary[x, y, cut].astype(F32))
                    phi[x, y, cut] = potential
                else:
                    potential = phi[x, y, cut]
                fields = [messages[e, x, y, cut].astype(F32) for e in range(6)]
                products = leave_one_out(potential, fields)
                for e in range(6):
                    store[OPPOSE[e], x, y, cut] = products[e].astype(BF16)

        return one

    def outgoing(store, scales, field, shifted):
        def one(x):
            for d in range(6):
                both = jnp.dot(
                    store[d, x].reshape(Y * Z, L), wide[d], preferred_element_type=F32
                )
                scale = L * recip(both[:, L:])
                scales[d, x] = scale.reshape(Y, Z, L)
                normal = (both[:, :L] * scale).reshape(Y, Z, L)
                field.plane(d, x)[...] = normal.astype(BF16)
                if d >= 4 and shifted:
                    for y in range(Y):
                        edge = Z - 1 if d == 4 else 0
                        nzo[d - 4, pl.ds(x * Y + y, 1)] = normal[y, edge:edge + 1]
                        nzs[d - 4, x, y] = pltpu.roll(
                            normal[y], 1 if d == 4 else Z - 1, 0
                        ).astype(BF16)

        return one

    def belief(x, y):
        spot = pl.ds(x * Y + y, 1)
        for c, cut in enumerate(cuts):
            fields = [N.at_shifted(d, x, y)[cut].astype(F32) for d in range(4)]
            row = lax.broadcasted_iota(jnp.int32, (CHUNK, L), 0)
            low = nzs[0, x, y, cut].astype(F32)
            if c == 0:
                low = jnp.where(row == 0, nzh[0, spot].astype(BF16).astype(F32), low)
            high = nzs[1, x, y, cut].astype(F32)
            if c == last:
                high = jnp.where(row == CHUNK - 1, nzh[1, spot].astype(BF16).astype(F32), high)
            fields += [low, high]
            before = [phi[x, y, cut]]
            for e in range(6):
                before.append(before[-1] * fields[e])
            joint = before[6]
            target_grad = cot[x, y, cut]
            scale = recip(jnp.sum(joint, axis=-1, keepdims=True))
            mean = jnp.sum(target_grad * joint, axis=-1, keepdims=True) * scale
            grad = (target_grad - mean) * (L * scale)
            out[x, y, cut] = grad * joint
            after = grad
            for e in range(5, -1, -1):
                value = before[e] * after
                A.at_own(e, x, y)[cut] = value.astype(BF16)
                if e == 4 and c == 0:
                    azo[0, spot] = value[0:1]
                if e == 5 and c == last:
                    azo[1, spot] = value[CHUNK - 1:CHUNK]
                after = after * fields[e]

    def grad_out(field, local, scales):
        def one(x, y):
            row = lax.broadcasted_iota(jnp.int32, (Z, L), 0)
            spot = pl.ds(x * Y + y, 1)
            grads, inners = [], []
            for d in range(6):
                if d < 4:
                    grad = field.at_shifted(d, x, y)[...].astype(F32)
                else:
                    value = field.z[d - 4, x, y].astype(F32)
                    halo = field.zhalo[d - 4, spot]
                    if d == 4:
                        grad = jnp.where(row == Z - 1, halo, pltpu.roll(value, Z - 1, 0))
                    else:
                        grad = jnp.where(row == 0, halo, pltpu.roll(value, 1, 0))
                part = (grad * local.at_own(d, x, y)[...].astype(F32)).astype(BF16)
                grads.append(grad)
                inners.append(jnp.dot(part, mean[...], preferred_element_type=F32))
            for d in range(6):
                local.at_own(d, x, y)[...] = (
                    scales[d, x, y] * (grads[d] - inners[d])
                ).astype(BF16)

        return one

    def weight_terms(store, local):
        def one(x):
            for d in range(6):
                acc[d] += lax.dot_general(
                    store[d, x].reshape(Y * Z, L), local.plane(d, x)[...].reshape(Y * Z, L),
                    (((0,), (0,)), ((), ())), preferred_element_type=F32,
                )

        return one

    def hidden_terms(x, local):
        for d in range(6):
            hidden_grad[d] = lax.dot_general(
                local.plane(d, x)[...].reshape(Y * Z, L), psib[d], (((1,), (1,)), ((), ())),
                preferred_element_type=F32,
            ).reshape(Y, Z, L)

    def adjoint(messages, field):
        def one(x, y):
            spot = pl.ds(x * Y + y, 1)
            for c, cut in enumerate(cuts):
                fields = [messages[e, x, y, cut].astype(F32) for e in range(6)]
                grads = [hidden_grad[OPPOSE[e], y, cut] for e in range(6)]
                before = [phi[x, y, cut]]
                slope = [None]
                for e in range(6):
                    part = before[e] * grads[e]
                    slope.append(part if e == 0 else slope[e] * fields[e] + part)
                    before.append(before[e] * fields[e] if e < 5 else None)
                out[x, y, cut] += slope[6]
                if field is None:
                    continue
                after, fall = None, None
                for e in range(5, -1, -1):
                    if e == 5:
                        value = slope[5]
                        after, fall = fields[5], grads[5]
                    else:
                        value = before[e] * fall
                        if e:
                            value = value + slope[e] * after
                            fall = fall * fields[e] + after * grads[e]
                            after = after * fields[e]
                    field.at_own(e, x, y)[cut] = value.astype(BF16)
                    if e == 4 and c == 0:
                        field.zsend[0, spot] = value[0:1]
                    if e == 5 and c == last:
                        field.zsend[1, spot] = value[CHUNK - 1:CHUNK]

        return one

    if early:
        hb_one, inv_one = more[0], more[1]
        local_one = Flat(more[2])
    else:
        hb_one, inv_one, local_one = hb, inv, N
    acc[...] = jnp.zeros_like(acc)
    loads[0].wait()
    loads[1].wait()
    one = exchange(N, 0)
    columns(*rims, hidden(second, hb, True), stride=X - 1)
    planes(*rims, outgoing(hb, inv, N, True), stride=X - 1)
    pl.semaphore_wait(barrier, group + others - 2)
    start(one, N, 1.0, range(2))
    columns(*inside, hidden(second, hb, True))
    planes(*inside, outgoing(hb, inv, N, True))
    start(one, N, 1.0, range(2, 6))
    loads[3].wait()
    if early:
        columns(0, X, hidden(first, hb_one, False))
    loads[2].wait()
    wait_recv(one[2:])
    columns(*inside, belief, width=2)
    wait_recv(one[:2])
    columns(*rims, belief, stride=X - 1, width=2)
    two = exchange(A, 1)
    start(two, A, 0.0, range(6))
    if early:
        planes(0, X, outgoing(hb_one, inv_one, local_one, False))
    wait_send(one)

    def second_back(x):
        each = grad_out(A, N, inv)
        lax.fori_loop(0, Y, lambda y, carry: (each(x, y), carry)[1], 0)
        hidden_terms(x, N)
        combine = adjoint(second, B)
        lax.fori_loop(0, Y, lambda y, carry: (combine(x, y), carry)[1], 0)

    wait_recv(two[2:])
    planes(*inside, second_back)
    wait_recv(two[:2])
    planes(*rims, second_back, stride=X - 1)
    three = exchange(B, 2)
    start(three, B, 0.0, range(6))
    planes(0, X, weight_terms(hb, N))
    wait_send(two)

    if not early:
        columns(0, X, hidden(first, hb_one, False))
        planes(0, X, outgoing(hb_one, inv_one, local_one, False))
    wait_recv(three[2:])
    columns(*inside, grad_out(B, local_one, inv_one))
    wait_recv(three[:2])
    columns(*rims, grad_out(B, local_one, inv_one), stride=X - 1)
    planes(0, X, weight_terms(hb_one, local_one))
    wait_send(three)

    def first_back(x):
        hidden_terms(x, local_one)
        combine = adjoint(first, None)
        lax.fori_loop(0, Y, lambda y, carry: (combine(x, y), carry)[1], 0)

    rs_src[...] = acc[...].reshape(group, rows, L).astype(BF16)
    scatters = []
    for k in range(1, group):
        goal = (mine + k) % group
        scatters.append(
            pltpu.make_async_remote_copy(
                src_ref=rs_src.at[goal], dst_ref=rs_recv.at[k - 1],
                send_sem=rs_send.at[k - 1], recv_sem=rs_recv_sem.at[k - 1],
                device_id=member(goal), device_id_type=MESH,
            )
        )
    for copy in scatters:
        copy.start()
    planes(0, X // 2, first_back)
    total = rs_src[mine].astype(F32)
    for k, copy in enumerate(scatters):
        copy.wait_recv()
        total = total + rs_recv[k].astype(F32)
    os_buf[me[other]] = total.astype(BF16)
    trades = []
    for k in range(1, others):
        goal = (me[other] + k) % others
        source = (me[other] + others - k) % others
        here = pltpu.make_async_remote_copy(
            src_ref=os_buf.at[me[other]], dst_ref=os_buf.at[me[other]],
            send_sem=os_send.at[k - 1], recv_sem=os_recv_sem.at[k - 1],
            device_id=target(**{other: goal}), device_id_type=MESH,
        )
        trades.append(here)
    for copy in trades:
        copy.start()
    planes(X // 2, X // 2 + X // 4, first_back)
    for copy in trades:
        copy.wait_recv()
    total = os_buf[0].astype(F32)
    for k in range(1, others):
        total = total + os_buf[k].astype(F32)
    ag_buf[mine] = total.astype(BF16)
    gathers = []
    for k in range(1, group):
        gathers.append(
            pltpu.make_async_remote_copy(
                src_ref=ag_buf.at[mine], dst_ref=ag_buf.at[mine],
                send_sem=ag_send.at[k - 1], recv_sem=ag_recv_sem.at[k - 1],
                device_id=member((mine + k) % group), device_id_type=MESH,
            )
        )
    for copy in gathers:
        copy.start()
    planes(X // 2 + X // 4, X, first_back)
    store = pltpu.make_async_copy(out, out_h, in_sem.at[4])
    store.start()
    for copy in gathers:
        copy.wait_recv()
    grad_compat[...] = jnp.exp(compat[...]) * ag_buf[...].astype(F32).reshape(6, L, L)
    for copy in scatters + trades + gathers:
        copy.wait_send()
    store.wait()


def body(sizes, unary, compat, saved_first, saved_second, cotangent):
    X, Y, Z, L = unary.shape
    scatter, other = ("gx", "gz"), "gy"
    if (6 * L) % (16 * sizes["gx"] * sizes["gz"]):
        scatter, other = ("gy", "gz"), "gx"
    group = sizes[scatter[0]] * sizes[scatter[1]]
    others = sizes[other]
    rows = 6 * L // group
    field = (X, Y, Z, L)
    early = X * Y * Z * L <= 384 * 1024
    more = [
        pltpu.VMEM((6,) + field, BF16),
        pltpu.VMEM((6,) + field, F32),
        pltpu.VMEM((6,) + field, BF16),
    ] if early else []

    def halo_set(extra):
        return [
            pltpu.VMEM((2, X + 1, Y, Z, L), BF16),
            pltpu.VMEM((2, X, Y + 1, Z, L), BF16),
            pltpu.VMEM((2, X, Y, Z, L), BF16),
        ] + extra + [pltpu.VMEM((2, X * Y, L), F32), pltpu.VMEM((2, X * Y, L), F32)]

    dma = pltpu.SemaphoreType.DMA
    return pl.pallas_call(
        functools.partial(kernel, early, sizes, scatter, other),
        out_shape=(
            jax.ShapeDtypeStruct(field, F32),
            jax.ShapeDtypeStruct((6, L, L), F32),
        ),
        in_specs=[
            pl.BlockSpec(memory_space=pl.ANY),
            pl.BlockSpec(memory_space=pltpu.VMEM),
            pl.BlockSpec(memory_space=pl.ANY),
            pl.BlockSpec(memory_space=pl.ANY),
            pl.BlockSpec(memory_space=pl.ANY),
        ],
        out_specs=(pl.BlockSpec(memory_space=pl.ANY), pl.BlockSpec(memory_space=pltpu.VMEM)),
        scratch_shapes=[
            pltpu.VMEM(field, BF16),
            pltpu.VMEM((6,) + field, BF16),
            pltpu.VMEM((6,) + field, BF16),
            pltpu.VMEM(field, F32),
            pltpu.VMEM(field, F32),
            pltpu.VMEM(field, F32),
            pltpu.VMEM((6,) + field, BF16),
            pltpu.VMEM((6,) + field, F32),
            pltpu.VMEM((6, Y, Z, L), F32),
            pltpu.VMEM((6, L, L), F32),
            pltpu.VMEM((6, L, L), BF16),
            pltpu.VMEM((6, L, 2 * L), BF16),
        ]
        + halo_set([pltpu.VMEM((2, X, Y, Z, L), BF16)])
        + halo_set([])
        + halo_set([])
        + [
            pltpu.VMEM((group, rows, L), BF16),
            pltpu.VMEM((group - 1, rows, L), BF16),
            pltpu.VMEM((others, rows, L), BF16),
            pltpu.VMEM((group, rows, L), BF16),
            pltpu.VMEM((L, L), BF16),
            dma((5,)),
            dma((3, 6)),
            dma((3, 6)),
            dma((group - 1,)),
            dma((group - 1,)),
            dma((others - 1,)),
            dma((others - 1,)),
            dma((group - 1,)),
            dma((group - 1,)),
        ]
        + more,
        compiler_params=pltpu.CompilerParams(
            collective_id=0, has_side_effects=True, vmem_limit_bytes=64 * 1024 * 1024 - 65536
        ),
    )(unary, compat, saved_first, saved_second, cotangent)


def solution(mesh):
    sizes = dict(mesh.shape)
    placed = (
        P("gx", "gy", "gz", None),
        P(),
        P(None, "gx", "gy", "gz", None),
        P(None, "gx", "gy", "gz", None),
        P("gx", "gy", "gz", None),
    )
    return jax.shard_map(
        functools.partial(body, sizes),
        mesh=mesh,
        in_specs=placed,
        out_specs=(P("gx", "gy", "gz", None), P()),
        check_vma=False,
    )
```

```python
import functools

import jax
import jax.numpy as jnp
from jax import lax
from jax.experimental import pallas as pl
from jax.experimental.pallas import tpu as pltpu
from jax.sharding import PartitionSpec as P

OPPOSE = (1, 0, 3, 2, 5, 4)
AXES = ("gx", "gy", "gz")
MESH = pl.DeviceIdType.MESH
F32 = jnp.float32
BF16 = jnp.bfloat16
CHUNK = 16


def recip(value):
    guess = pl.reciprocal(value, approx=True)
    return guess * (2.0 - value * guess)


def leave_one_out(start, fields):
    before = [start]
    for index in range(5):
        before.append(before[-1] * fields[index])
    after = fields[5]
    result = [None] * 6
    result[5] = before[5]
    for index in range(4, -1, -1):
        result[index] = before[index] * after
        if index:
            after = after * fields[index]
    return result


class Halo:
    def __init__(self, x_ref, y_ref, z_ref, zhalo_ref, zsend_ref, forward, shape):
        self.x, self.y, self.z, self.zhalo, self.zsend = x_ref, y_ref, z_ref, zhalo_ref, zsend_ref
        self.shape = shape
        self.step = [(-1 if d % 2 == 0 else 1) * (1 if forward else -1) for d in range(6)]

    def own(self, d):
        return 1 if self.step[d] < 0 else 0

    def read(self, d):
        return 0 if self.step[d] < 0 else 1

    def at_own(self, d, x, y):
        if d < 2:
            return self.x.at[d, x + self.own(d), y]
        if d < 4:
            return self.y.at[d - 2, x, y + self.own(d)]
        return self.z.at[d - 4, x, y]

    def at_shifted(self, d, x, y):
        if d < 2:
            return self.x.at[d, x + self.read(d), y]
        return self.y.at[d - 2, x, y + self.read(d)]

    def plane(self, d, x):
        X, Y, Z, L = self.shape
        if d < 2:
            return self.x.at[d, x + self.own(d)]
        if d < 4:
            return self.y.at[d - 2, x, pl.ds(self.own(d), Y)]
        return self.z.at[d - 4, x]

    def halo(self, d):
        X, Y, Z, L = self.shape
        if d < 2:
            return self.x.at[d, 0 if self.step[d] < 0 else X]
        if d < 4:
            return self.y.at[d - 2, :, 0 if self.step[d] < 0 else Y]
        return self.zhalo.at[d - 4]

    def face(self, d):
        X, Y, Z, L = self.shape
        if d < 2:
            return self.x.at[d, X if self.step[d] < 0 else 0]
        if d < 4:
            return self.y.at[d - 2, :, Y if self.step[d] < 0 else 0]
        return self.zsend.at[d - 4]


class Flat:
    def __init__(self, ref):
        self.ref = ref

    def at_own(self, d, x, y):
        return self.ref.at[d, x, y]

    def plane(self, d, x):
        return self.ref.at[d, x]


def kernel(
    early, sizes, scatter, other,
    unary_h, compat, first_h, second_h, cot_h,
    out_h, grad_compat,
    unary, first, second, cot, phi, out, hb, inv, hidden_grad, acc, psib, wide,
    nx, ny, nz, nzs, nzh, nzo, ax, ay, az, azh, azo, bx, by, bz, bzh, bzo,
    rs_src, rs_recv, os_buf, ag_buf, mean,
    in_sem, send_sem, recv_sem, rs_send, rs_recv_sem, os_send, os_recv_sem, ag_send, ag_recv_sem,
    *more,
):
    X, Y, Z, L = shape = phi.shape
    me = {axis: lax.axis_index(axis) for axis in AXES}

    def target(**changed):
        return tuple(changed.get(axis, me[axis]) for axis in AXES)

    inner_count = sizes[scatter[1]]
    group = sizes[scatter[0]] * inner_count
    mine = me[scatter[0]] * inner_count + me[scatter[1]]
    others = sizes[other]
    rows = 6 * L // group

    def member(index):
        return target(**{scatter[0]: index // inner_count, scatter[1]: index % inner_count})

    loads = [
        pltpu.make_async_copy(src, dst, in_sem.at[i])
        for i, (src, dst) in enumerate(
            ((unary_h, unary), (second_h, second), (cot_h, cot), (first_h, first))
        )
    ]
    for load in loads:
        load.start()

    barrier = pltpu.get_barrier_semaphore()
    for k in range(1, group):
        pl.semaphore_signal(barrier, inc=1, device_id=member((mine + k) % group), device_id_type=MESH)
    for k in range(1, others):
        pl.semaphore_signal(
            barrier, inc=1, device_id=target(**{other: (me[other] + k) % others}), device_id_type=MESH
        )

    for d in range(6):
        rounded = jnp.exp(compat[d]).astype(BF16)
        psib[d] = rounded
        wide[d, :, :L] = rounded
        sums = jnp.sum(rounded.astype(F32), axis=1, keepdims=True)
        wide[d, :, L:] = jnp.broadcast_to(sums, (L, L)).astype(BF16)

    mean[...] = jnp.full((L, L), 1.0 / L, BF16)

    N = Halo(nx, ny, nz, nzh, nzo, True, shape)
    A = Halo(ax, ay, az, azh, azo, False, shape)
    B = Halo(bx, by, bz, bzh, bzo, False, shape)

    def exchange(field, number):
        plan = []
        for d in range(6):
            axis = AXES[d // 2]
            count = sizes[axis]
            place = me[axis]
            up = field.step[d] < 0
            goal = place + 1 if up else place - 1
            sends = place < count - 1 if up else place > 0
            gets = place > 0 if up else place < count - 1
            copy = pltpu.make_async_remote_copy(
                src_ref=field.face(d),
                dst_ref=field.halo(d),
                send_sem=send_sem.at[number, d],
                recv_sem=recv_sem.at[number, d],
                device_id=target(**{axis: goal}),
                device_id_type=MESH,
            )
            plan.append((sends, gets, copy))
        return plan

    def start(plan, field, value, which):
        for d in which:
            sends, gets, copy = plan[d]

            @pl.when(sends)
            def _():
                copy.start()

            @pl.when(jnp.logical_not(gets))
            def _():
                spot = field.halo(d)
                spot[...] = jnp.full(spot.shape, value, spot.dtype)

    def wait_recv(plan):
        for sends, gets, copy in plan:
            @pl.when(gets)
            def _():
                copy.wait_recv()

    def wait_send(plan):
        for sends, gets, copy in plan:
            @pl.when(sends)
            def _():
                copy.wait_send()

    def planes(lo, hi, step, stride=1):
        def one(x, carry):
            step(x * stride)
            return carry

        lax.fori_loop(lo, hi, one, 0)

    def columns(lo, hi, step, stride=1, width=1):
        pieces = Y // width

        def one(i, carry):
            for j in range(width):
                step((i // pieces) * stride, (i % pieces) * width + j)
            return carry

        lax.fori_loop(lo * pieces, hi * pieces, one, 0)

    inside, rims = (1, X - 1), (0, 2)

    cuts = [pl.ds(c * CHUNK, CHUNK) for c in range(Z // CHUNK)]
    last = len(cuts) - 1

    def hidden(messages, store, fresh):
        def one(x, y):
            for cut in cuts:
                if fresh:
                    potential = jnp.exp(unary[x, y, cut].astype(F32))
                    phi[x, y, cut] = potential
                else:
                    potential = phi[x, y, cut]
                fields = [messages[e, x, y, cut].astype(F32) for e in range(6)]
                products = leave_one_out(potential, fields)
                for e in range(6):
                    store[OPPOSE[e], x, y, cut] = products[e].astype(BF16)

        return one

    def outgoing(store, scales, field, shifted):
        def one(x):
            for d in range(6):
                both = jnp.dot(
                    store[d, x].reshape(Y * Z, L), wide[d], preferred_element_type=F32
                )
                scale = L * recip(both[:, L:])
                scales[d, x] = scale.reshape(Y, Z, L)
                normal = (both[:, :L] * scale).reshape(Y, Z, L)
                field.plane(d, x)[...] = normal.astype(BF16)
                if d >= 4 and shifted:
                    for y in range(Y):
                        edge = Z - 1 if d == 4 else 0
                        nzo[d - 4, pl.ds(x * Y + y, 1)] = normal[y, edge:edge + 1]
                        nzs[d - 4, x, y] = pltpu.roll(
                            normal[y], 1 if d == 4 else Z - 1, 0
                        ).astype(BF16)

        return one

    def belief(x, y):
        spot = pl.ds(x * Y + y, 1)
        for c, cut in enumerate(cuts):
            fields = [N.at_shifted(d, x, y)[cut].astype(F32) for d in range(4)]
            row = lax.broadcasted_iota(jnp.int32, (CHUNK, L), 0)
            low = nzs[0, x, y, cut].astype(F32)
            if c == 0:
                low = jnp.where(row == 0, nzh[0, spot].astype(BF16).astype(F32), low)
            high = nzs[1, x, y, cut].astype(F32)
            if c == last:
                high = jnp.where(row == CHUNK - 1, nzh[1, spot].astype(BF16).astype(F32), high)
            fields += [low, high]
            before = [phi[x, y, cut]]
            for e in range(6):
                before.append(before[-1] * fields[e])
            joint = before[6]
            target_grad = cot[x, y, cut]
            scale = recip(jnp.sum(joint, axis=-1, keepdims=True))
            mean = jnp.sum(target_grad * joint, axis=-1, keepdims=True) * scale
            grad = (target_grad - mean) * (L * scale)
            out[x, y, cut] = grad * joint
            after = grad
            for e in range(5, -1, -1):
                value = before[e] * after
                A.at_own(e, x, y)[cut] = value.astype(BF16)
                if e == 4 and c == 0:
                    azo[0, spot] = value[0:1]
                if e == 5 and c == last:
                    azo[1, spot] = value[CHUNK - 1:CHUNK]
                after = after * fields[e]

    def grad_out(field, local, scales):
        def one(x):
            row = lax.broadcasted_iota(jnp.int32, (Z, L), 0)
            for d in (0, 2, 4, 1, 3, 5):
                if d < 2:
                    grad = field.x[d, x + field.read(d)].astype(F32)
                elif d < 4:
                    grad = field.y[d - 2, x, pl.ds(field.read(d), Y)].astype(F32)
                else:
                    grad = []
                    for y in range(Y):
                        value = field.z[d - 4, x, y].astype(F32)
                        halo = field.zhalo[d - 4, pl.ds(x * Y + y, 1)]
                        if d == 4:
                            grad.append(jnp.where(row == Z - 1, halo, pltpu.roll(value, Z - 1, 0)))
                        else:
                            grad.append(jnp.where(row == 0, halo, pltpu.roll(value, 1, 0)))
                    grad = jnp.stack(grad)
                part = (grad * local.plane(d, x)[...].astype(F32)).astype(BF16)
                inner = jnp.dot(
                    part.reshape(Y * Z, L), mean[...], preferred_element_type=F32
                ).reshape(Y, Z, L)
                local.plane(d, x)[...] = (scales[d, x] * (grad - inner)).astype(BF16)

        return one

    def weight_terms(store, local):
        def one(x):
            for d in range(6):
                acc[d] += lax.dot_general(
                    store[d, x].reshape(Y * Z, L), local.plane(d, x)[...].reshape(Y * Z, L),
                    (((0,), (0,)), ((), ())), preferred_element_type=F32,
                )

        return one

    def hidden_terms(x, local):
        for d in range(6):
            hidden_grad[d] = lax.dot_general(
                local.plane(d, x)[...].reshape(Y * Z, L), psib[d], (((1,), (1,)), ((), ())),
                preferred_element_type=F32,
            ).reshape(Y, Z, L)

    def adjoint(messages, field):
        def one(x, y):
            spot = pl.ds(x * Y + y, 1)
            for c, cut in enumerate(cuts):
                fields = [messages[e, x, y, cut].astype(F32) for e in range(6)]
                grads = [hidden_grad[OPPOSE[e], y, cut] for e in range(6)]
                before = [phi[x, y, cut]]
                slope = [None]
                for e in range(6):
                    part = before[e] * grads[e]
                    slope.append(part if e == 0 else slope[e] * fields[e] + part)
                    before.append(before[e] * fields[e] if e < 5 else None)
                out[x, y, cut] += slope[6]
                if field is None:
                    continue
                after, fall = None, None
                for e in range(5, -1, -1):
                    if e == 5:
                        value = slope[5]
                        after, fall = fields[5], grads[5]
                    else:
                        value = before[e] * fall
                        if e:
                            value = value + slope[e] * after
                            fall = fall * fields[e] + after * grads[e]
                            after = after * fields[e]
                    field.at_own(e, x, y)[cut] = value.astype(BF16)
                    if e == 4 and c == 0:
                        field.zsend[0, spot] = value[0:1]
                    if e == 5 and c == last:
                        field.zsend[1, spot] = value[CHUNK - 1:CHUNK]

        return one

    if early:
        hb_one, inv_one = more[0], more[1]
        local_one = Flat(more[2])
    else:
        hb_one, inv_one, local_one = hb, inv, N
    acc[...] = jnp.zeros_like(acc)
    loads[0].wait()
    loads[1].wait()
    one = exchange(N, 0)
    columns(*rims, hidden(second, hb, True), stride=X - 1)
    planes(*rims, outgoing(hb, inv, N, True), stride=X - 1)
    pl.semaphore_wait(barrier, group + others - 2)
    start(one, N, 1.0, range(2))
    columns(*inside, hidden(second, hb, True))
    planes(*inside, outgoing(hb, inv, N, True))
    start(one, N, 1.0, range(2, 6))
    loads[3].wait()
    if early:
        columns(0, X, hidden(first, hb_one, False))
    loads[2].wait()
    wait_recv(one[2:])
    columns(*inside, belief, width=2)
    wait_recv(one[:2])
    columns(*rims, belief, stride=X - 1, width=2)
    two = exchange(A, 1)
    start(two, A, 0.0, range(6))
    if early:
        planes(0, X, outgoing(hb_one, inv_one, local_one, False))
    wait_send(one)

    def second_back(x):
        grad_out(A, N, inv)(x)
        hidden_terms(x, N)
        combine = adjoint(second, B)
        lax.fori_loop(0, Y, lambda y, carry: (combine(x, y), carry)[1], 0)

    wait_recv(two[2:])
    planes(*inside, second_back)
    wait_recv(two[:2])
    planes(*rims, second_back, stride=X - 1)
    three = exchange(B, 2)
    start(three, B, 0.0, range(6))
    planes(0, X, weight_terms(hb, N))
    wait_send(two)

    if not early:
        columns(0, X, hidden(first, hb_one, False))
        planes(0, X, outgoing(hb_one, inv_one, local_one, False))
    wait_recv(three[2:])
    planes(*inside, grad_out(B, local_one, inv_one))
    wait_recv(three[:2])
    planes(*rims, grad_out(B, local_one, inv_one), stride=X - 1)
    planes(0, X, weight_terms(hb_one, local_one))
    wait_send(three)

    def first_back(x):
        hidden_terms(x, local_one)
        combine = adjoint(first, None)
        lax.fori_loop(0, Y, lambda y, carry: (combine(x, y), carry)[1], 0)

    rs_src[...] = acc[...].reshape(group, rows, L).astype(BF16)
    scatters = []
    for k in range(1, group):
        goal = (mine + k) % group
        scatters.append(
            pltpu.make_async_remote_copy(
                src_ref=rs_src.at[goal], dst_ref=rs_recv.at[k - 1],
                send_sem=rs_send.at[k - 1], recv_sem=rs_recv_sem.at[k - 1],
                device_id=member(goal), device_id_type=MESH,
            )
        )
    for copy in scatters:
        copy.start()
    planes(0, X // 2, first_back)
    total = rs_src[mine].astype(F32)
    for k, copy in enumerate(scatters):
        copy.wait_recv()
        total = total + rs_recv[k].astype(F32)
    os_buf[me[other]] = total.astype(BF16)
    trades = []
    for k in range(1, others):
        goal = (me[other] + k) % others
        source = (me[other] + others - k) % others
        here = pltpu.make_async_remote_copy(
            src_ref=os_buf.at[me[other]], dst_ref=os_buf.at[me[other]],
            send_sem=os_send.at[k - 1], recv_sem=os_recv_sem.at[k - 1],
            device_id=target(**{other: goal}), device_id_type=MESH,
        )
        trades.append(here)
    for copy in trades:
        copy.start()
    planes(X // 2, X // 2 + X // 4, first_back)
    for copy in trades:
        copy.wait_recv()
    total = os_buf[0].astype(F32)
    for k in range(1, others):
        total = total + os_buf[k].astype(F32)
    ag_buf[mine] = total.astype(BF16)
    gathers = []
    for k in range(1, group):
        gathers.append(
            pltpu.make_async_remote_copy(
                src_ref=ag_buf.at[mine], dst_ref=ag_buf.at[mine],
                send_sem=ag_send.at[k - 1], recv_sem=ag_recv_sem.at[k - 1],
                device_id=member((mine + k) % group), device_id_type=MESH,
            )
        )
    for copy in gathers:
        copy.start()
    planes(X // 2 + X // 4, X, first_back)
    store = pltpu.make_async_copy(out, out_h, in_sem.at[4])
    store.start()
    for copy in gathers:
        copy.wait_recv()
    grad_compat[...] = jnp.exp(compat[...]) * ag_buf[...].astype(F32).reshape(6, L, L)
    for copy in scatters + trades + gathers:
        copy.wait_send()
    store.wait()


def body(sizes, unary, compat, saved_first, saved_second, cotangent):
    X, Y, Z, L = unary.shape
    scatter, other = ("gx", "gz"), "gy"
    if (6 * L) % (16 * sizes["gx"] * sizes["gz"]):
        scatter, other = ("gy", "gz"), "gx"
    group = sizes[scatter[0]] * sizes[scatter[1]]
    others = sizes[other]
    rows = 6 * L // group
    field = (X, Y, Z, L)
    early = X * Y * Z * L <= 384 * 1024
    more = [
        pltpu.VMEM((6,) + field, BF16),
        pltpu.VMEM((6,) + field, F32),
        pltpu.VMEM((6,) + field, BF16),
    ] if early else []

    def halo_set(extra):
        return [
            pltpu.VMEM((2, X + 1, Y, Z, L), BF16),
            pltpu.VMEM((2, X, Y + 1, Z, L), BF16),
            pltpu.VMEM((2, X, Y, Z, L), BF16),
        ] + extra + [pltpu.VMEM((2, X * Y, L), F32), pltpu.VMEM((2, X * Y, L), F32)]

    dma = pltpu.SemaphoreType.DMA
    return pl.pallas_call(
        functools.partial(kernel, early, sizes, scatter, other),
        out_shape=(
            jax.ShapeDtypeStruct(field, F32),
            jax.ShapeDtypeStruct((6, L, L), F32),
        ),
        in_specs=[
            pl.BlockSpec(memory_space=pl.ANY),
            pl.BlockSpec(memory_space=pltpu.VMEM),
            pl.BlockSpec(memory_space=pl.ANY),
            pl.BlockSpec(memory_space=pl.ANY),
            pl.BlockSpec(memory_space=pl.ANY),
        ],
        out_specs=(pl.BlockSpec(memory_space=pl.ANY), pl.BlockSpec(memory_space=pltpu.VMEM)),
        scratch_shapes=[
            pltpu.VMEM(field, BF16),
            pltpu.VMEM((6,) + field, BF16),
            pltpu.VMEM((6,) + field, BF16),
            pltpu.VMEM(field, F32),
            pltpu.VMEM(field, F32),
            pltpu.VMEM(field, F32),
            pltpu.VMEM((6,) + field, BF16),
            pltpu.VMEM((6,) + field, F32),
            pltpu.VMEM((6, Y, Z, L), F32),
            pltpu.VMEM((6, L, L), F32),
            pltpu.VMEM((6, L, L), BF16),
            pltpu.VMEM((6, L, 2 * L), BF16),
        ]
        + halo_set([pltpu.VMEM((2, X, Y, Z, L), BF16)])
        + halo_set([])
        + halo_set([])
        + [
            pltpu.VMEM((group, rows, L), BF16),
            pltpu.VMEM((group - 1, rows, L), BF16),
            pltpu.VMEM((others, rows, L), BF16),
            pltpu.VMEM((group, rows, L), BF16),
            pltpu.VMEM((L, L), BF16),
            dma((5,)),
            dma((3, 6)),
            dma((3, 6)),
            dma((group - 1,)),
            dma((group - 1,)),
            dma((others - 1,)),
            dma((others - 1,)),
            dma((group - 1,)),
            dma((group - 1,)),
        ]
        + more,
        compiler_params=pltpu.CompilerParams(
            collective_id=0, has_side_effects=True, vmem_limit_bytes=64 * 1024 * 1024 - 65536
        ),
    )(unary, compat, saved_first, saved_second, cotangent)


def solution(mesh):
    sizes = dict(mesh.shape)
    placed = (
        P("gx", "gy", "gz", None),
        P(),
        P(None, "gx", "gy", "gz", None),
        P(None, "gx", "gy", "gz", None),
        P("gx", "gy", "gz", None),
    )
    return jax.shard_map(
        functools.partial(body, sizes),
        mesh=mesh,
        in_specs=placed,
        out_specs=(P("gx", "gy", "gz", None), P()),
        check_vma=False,
    )
```
